512 devices in a mesh: seq: 512 (over x, y, z, core).
Axes of the slice: x: 4, y: 8, z: 8, core: 2. Of those that a mesh axis runs over, the one named last changes fastest.
Arguments:
- queries: bfloat16 [262144, 1024], P('seq'), may hold values from -60 to 60
- keys: bfloat16 [262144, 1024], P('seq'), may hold values from -60 to 60
- values: bfloat16 [262144, 1024], P('seq'), may hold values from -6 to 6
- lengths: int32 [512], P('seq'), may hold values from 64 to 512
Outputs:
- attended: bfloat16 [262144, 1024], P('seq')
The draws below stay inside these ranges and needn't reach their ends.
All inputs are finite; a program needn't handle non-finite values.
Results may differ from the reference program's by a relative error of at most 0.0056.
Values may be sent and summed in bfloat16 or wider, within the bound.
A program may use at most 64 MiB of HBM per device.

```python
import math
import jax
import jax.numpy as jnp
from jax import lax

D = 1024
HEADS = 16
HEAD_DIM = 64
TOK_DEV = 512
NBLOCKS = 512
OFFSET = 128
TOKENS = 262144


def shared_field(key):
    return jax.random.normal(key, (TOKENS, D), jnp.float32)


def draw_keys(key, part):
    base_field = shared_field(key)
    return base_field.astype(jnp.bfloat16)


def draw_queries(key, part):
    key = jax.random.fold_in(key, 1)
    fresh = jax.random.normal(key, (TOKENS, D), jnp.float32)
    return fresh.astype(jnp.bfloat16)


def with_ends(drawn, own_key, low, high):
    longest = drawn.shape.index(max(drawn.shape))
    spots = []
    for shift in (0, 1):
        where = [jax.random.randint(jax.random.fold_in(own_key, axis), (), 0, length) for axis, length in enumerate(drawn.shape)]
        where[longest] = (where[longest] + shift) % drawn.shape[longest]
        spots.append(tuple(where))
    return drawn.at[spots[0]].set(low).at[spots[1]].set(high)


def shard_levels(rng, extent, cuts, low, top_value):
    level, own = 1.0, jax.random.fold_in(rng, 6)
    for dim, shards_of in cuts:
        draws = jnp.exp(jax.random.uniform(jax.random.fold_in(own, dim), (shards_of,), jnp.float32, low / len(cuts), top_value / len(cuts)))
        level = level * jnp.repeat(draws, extent[dim] // shards_of).reshape([-1 if axis == dim else 1 for axis in range(len(extent))])
    return level


def scatter_about(own_key, extent, spread, bound, split=(), held_as=jnp.bfloat16):
    array = jax.random.normal(own_key, extent, jnp.float32) * spread
    if len(split) > 0:
        array = shard_levels(own_key, extent, split, -0.22, 0.18) * array
    return jnp.clip(array, min=-bound, max=bound).astype(held_as)


def setup_inputs(seed: int = 0) -> dict:
    seeds = jax.random.split(jax.random.key(seed), 5)
    queries = draw_queries(jax.random.fold_in(seeds[4], 71), 0)
    keys = draw_keys(jax.random.fold_in(seeds[4], 71), 0)
    values = scatter_about(seeds[2], (TOKENS, D), 1.0, 6.0, ((0, 512),))
    lengths = with_ends(jax.random.randint(seeds[3], (NBLOCKS,), TOK_DEV // 8, TOK_DEV + 1), jax.random.fold_in(seeds[3], 1), TOK_DEV // 8, TOK_DEV).astype(jnp.int32)
    return dict(queries=queries, keys=keys, values=values, lengths=lengths)


def attend_block(query_block, key_block, value_block, length):
    row_count = query_block.shape[0]
    key_count = key_block.shape[0]
    query_heads = query_block.astype(jnp.float32).reshape(row_count, HEADS, HEAD_DIM)
    key_heads = key_block.astype(jnp.float32).reshape(key_count, HEADS, HEAD_DIM)
    value_heads = value_block.astype(jnp.float32).reshape(key_count, HEADS, HEAD_DIM)
    scores = jnp.einsum('thd,shd->hts', query_heads, key_heads) * (1.0 / math.sqrt(HEAD_DIM))
    visible = jnp.arange(key_count) < length
    scores = jnp.where(visible[None, None, :], scores, -1e+30)
    row_peaks = lax.optimization_barrier(jnp.max(scores, axis=-1))
    weights = jnp.exp(scores - row_peaks[..., None]).astype(jnp.bfloat16)
    weights = lax.optimization_barrier(weights).astype(jnp.float32)
    totals = lax.optimization_barrier(jnp.sum(weights, axis=-1))
    blended = jnp.einsum('hts,shd->thd', weights, value_heads) / jnp.transpose(totals)[:, :, None]
    return (blended.reshape(row_count, HEADS * HEAD_DIM).astype(jnp.bfloat16), row_peaks + jnp.log(totals))

def combine(partials):
    log_sums = jnp.stack([partial_value[1] for partial_value in partials])
    ceiling = lax.optimization_barrier(jnp.max(log_sums, axis=0))
    shares = jnp.exp(log_sums - ceiling[None])
    share_total = lax.optimization_barrier(jnp.sum(shares, axis=0))
    row_count = partials[0][0].shape[0]
    mixture = jnp.zeros((row_count, HEADS, HEAD_DIM), jnp.float32)
    for position, partial_value in enumerate(partials):
        piece_heads = partial_value[0].astype(jnp.float32).reshape(row_count, HEADS, HEAD_DIM)
        mixture = mixture + piece_heads * jnp.transpose(shares[position])[:, :, None]
    mixture = mixture / jnp.transpose(share_total)[:, :, None]
    return mixture.reshape(row_count, HEADS * HEAD_DIM).astype(jnp.bfloat16)

def reference(queries, keys, values, lengths):
    query_blocks = queries.reshape(NBLOCKS, TOK_DEV, D)
    key_blocks = keys.reshape(NBLOCKS, TOK_DEV, D)
    value_blocks = values.reshape(NBLOCKS, TOK_DEV, D)

    def one_block(block_index):
        partials = []
        for block_shift in (0, -1, 1, -OFFSET, OFFSET):
            source = ((block_index + block_shift) % NBLOCKS).astype(jnp.int32)
            partials.append(attend_block(query_blocks[block_index], key_blocks[source], value_blocks[source], lengths[source]))
        return combine(partials)
    result = lax.map(one_block, jnp.arange(NBLOCKS, dtype=jnp.int32))
    return result.reshape(TOKENS, D)
```

```python
import functools
import math

import jax
import jax.numpy as jnp
from jax import lax
from jax.experimental import pallas as pl
from jax.experimental.pallas import tpu as pltpu
from jax.sharding import PartitionSpec as P

MESH = pl.DeviceIdType.MESH
HEAD_DIM = 64
LANES = 128
PLANE = 128
RELAYS = 16
HOP_STEP = (5, 4)
UP, DOWN, SAME, OFF = range(4)
GAIN = math.log2(math.e) / math.sqrt(HEAD_DIM)
BF16 = jnp.bfloat16
F32 = jnp.float32


RELAY_AT = (
    (2, 1, 1), (5, 1, 1), (7, 6, 1), (6, 0, 1), (1, 0, 1), (6, 6, 1), (7, 5, 1), (4, 1, 1),
    (0, 0, 1), (5, 0, 1), (0, 1, 1), (5, 6, 1), (2, 0, 1), (6, 1, 1), (3, 0, 1), (4, 0, 1),
)


def relay_place(flow, g):
    y, z, core = RELAY_AT[g]
    place = (y * 8 + z) * 2 + core
    return place if flow == 0 else PLANE - 1 - place


def kernel(
    count, len_ref, q_hbm, k_hbm, v_hbm, out_hbm,
    q_own, kv_own, kv_in, out_own, lens, bias, k_aug, v_aug, probs, acc, tot, peak, relay,
    own_sem, send_sem, recv_sem, len_send, len_recv, piece_sem, hop_recv, hop_send, out_sem, ready, off_ready,
):
    rows, width = q_own.shape
    strips = width // LANES
    me = lax.axis_index("seq")
    core = lax.rem(me, 2)
    place = lax.rem(me, PLANE)
    plane = me - place
    above = lax.rem(plane + PLANE, count)
    below = lax.rem(plane + count - PLANE, count)
    partners = [
        lax.rem(me + PLANE, count),
        lax.rem(me + count - PLANE, count),
        me + 1 - 2 * core,
        lax.rem(me + count - 1 + 2 * core, count),
    ]
    first, last = place == 0, place == PLANE - 1
    inner = jnp.logical_not(jnp.logical_or(first, last))
    is_relay, piece = [], []
    for flow in range(2):
        hits = [place == relay_place(flow, g) for g in range(RELAYS)]
        is_relay.append(functools.reduce(jnp.logical_or, hits))
        piece.append(sum(jnp.where(hit, g, 0) for g, hit in enumerate(hits)))

    def strip_of(j):
        if isinstance(j, int):
            return pl.ds(j * LANES, LANES)
        return pl.ds(pl.multiple_of(j * LANES, LANES), LANES)

    def remote(src, dst, send, recv, device):
        return pltpu.make_async_remote_copy(
            src_ref=src, dst_ref=dst, send_sem=send, recv_sem=recv, device_id=(device,), device_id_type=MESH
        )

    def strip_copy(slot, t, j):
        src = (k_hbm, v_hbm)[t]
        return remote(
            src.at[:, strip_of(j)], kv_in.at[slot, t, :, strip_of(j)],
            send_sem.at[slot, t, j], recv_sem.at[slot, t, j], partners[slot],
        )

    def len_copy(slot):
        return remote(lens.at[4], lens.at[slot], len_send.at[slot], len_recv.at[slot], partners[slot])

    def piece_copy(flow, g):
        src = (k_hbm, v_hbm)[g % 2]
        return remote(
            src.at[:, strip_of(g // 2)], relay.at[flow], piece_sem.at[g], hop_recv.at[flow],
            (above, below)[flow] + relay_place(flow, g),
        )

    def hop_copy(flow):
        t, j = lax.rem(piece[flow], 2), lax.div(piece[flow], 2)
        return remote(
            relay.at[flow], kv_in.at[OFF, t, :, strip_of(j)], hop_send.at[flow], recv_sem.at[OFF, t, j],
            plane + (0, PLANE - 1)[flow],
        )

    def signal(semaphore, device):
        pl.semaphore_signal(semaphore, inc=1, device_id=(device,), device_id_type=MESH)

    local = [
        pltpu.make_async_copy(q_hbm, q_own, own_sem.at[0]),
        pltpu.make_async_copy(k_hbm, kv_own.at[0], own_sem.at[1]),
        pltpu.make_async_copy(v_hbm, kv_own.at[1], own_sem.at[2]),
    ]
    barrier = pltpu.get_barrier_semaphore()
    for slot in (UP, DOWN, SAME):
        signal(barrier, partners[slot])

    @pl.when(core == 0)
    def _():
        signal(barrier, partners[OFF])

    @pl.when(first)
    def _():
        for g in range(RELAYS):
            signal(barrier, plane + relay_place(0, g))
            signal(barrier, below + relay_place(1, g))

    @pl.when(last)
    def _():
        for g in range(RELAYS):
            signal(barrier, plane + relay_place(1, g))

    @pl.when(is_relay[0])
    def _():
        signal(barrier, below + PLANE - 1)

    for copy in local:
        copy.start()
    lens[4] = jnp.full(lens.shape[1:], len_ref[0], jnp.int32)
    pl.semaphore_wait(
        barrier,
        3 + core + jnp.where(last, RELAYS, 0) + jnp.where(is_relay[0], 1, 0) + jnp.where(is_relay[1], 2, 0),
    )

    @pl.when(core == 1)
    def _():
        signal(off_ready, partners[OFF])

    @pl.when(is_relay[1])
    def _():
        signal(ready, above)

    def start_pieces(flow):
        for g in range(RELAYS):
            piece_copy(flow, g).start()

    def start_off():
        len_copy(OFF).start()

        @pl.when(inner)
        def _():
            for j in range(strips):
                for t in range(2):
                    strip_copy(OFF, t, j).start()

    pl.when(last)(functools.partial(start_pieces, 0))
    for slot in (UP, DOWN, SAME):
        len_copy(slot).start()
    for j in range(strips):
        for slot in (UP, DOWN, SAME):
            for t in range(2):
                strip_copy(slot, t, j).start()
    pl.when(core == 1)(start_off)

    for copy in local:
        copy.wait()
    position = lax.broadcasted_iota(jnp.int32, (rows, LANES), 0)

    def take_mask(block):
        bias[block] = jnp.where(position < lens[block, 0:1, :], 0.0, -1e30).astype(BF16)

    take_mask(4)
    len_copy(SAME).wait_recv()
    take_mask(SAME)

    lane = lax.broadcasted_iota(jnp.int32, (rows, LANES), 1)
    low = lane < HEAD_DIM
    ones = jnp.ones((rows, LANES), BF16)
    marks = ((lane == HEAD_DIM).astype(BF16), (lane == 0).astype(BF16))

    def block_view(block, t, j):
        return kv_own[t, :, strip_of(j)] if block == 4 else kv_in[block, t, :, strip_of(j)]

    def take_keys(blocks, j):
        for i, block in enumerate(blocks):
            keys, mask = block_view(block, 0, j), bias[block]
            at = pl.ds(i * rows, rows)
            k_aug[0, at] = jnp.where(low, keys, mask)
            k_aug[1, at] = jnp.where(low, mask, keys)

    def take_values(blocks, j):
        for i, block in enumerate(blocks):
            values = block_view(block, 1, j)
            at = pl.ds(i * rows, rows)
            v_aug[0, at] = jnp.where(low, values, ones)
            v_aug[1, at] = jnp.where(low, ones, values)

    def score(head, n, j):
        q = q_own[:, strip_of(j)]
        q = jnp.where(low, q, marks[0]) if head == 0 else jnp.where(low, marks[1], q)
        return lax.dot_general(
            q, k_aug[head, 0 : n * rows], (((1,), (1,)), ((), ())), preferred_element_type=F32
        )

    def weigh(scores):
        top = jnp.max(scores, axis=1, keepdims=True)
        return jnp.exp2((scores - top) * GAIN).astype(BF16), top

    def blend(head, n, weights):
        return jnp.dot(weights, v_aug[head, 0 : n * rows], preferred_element_type=F32)

    def joined(pair, tops):
        blended = jnp.where(low, pair[0], pair[1])
        totals = pltpu.roll(jnp.where(low, pair[1], pair[0]), HEAD_DIM, 1)
        return blended, totals, jnp.where(low, tops[0], tops[1])

    def attend(blocks, j):
        take_keys(blocks, j)
        take_values(blocks, j)
        n = len(blocks)
        scores = [score(head, n, j) for head in range(2)]
        weights, tops = zip(*[weigh(s) for s in scores])
        return joined([blend(head, n, weights[head]) for head in range(2)], tops)

    def merged(j, blended, totals, top):
        ceiling = jnp.maximum(peak[j], top)
        old, new = jnp.exp2((peak[j] - ceiling) * GAIN), jnp.exp2((top - ceiling) * GAIN)
        return acc[j] * old + blended * new, tot[j] * old + totals * new, ceiling

    def keep(j, state):
        acc[j], tot[j], peak[j] = state

    def out_copy(j):
        return pltpu.make_async_copy(
            out_own.at[:, strip_of(j)], out_hbm.at[:, strip_of(j)], out_sem.at[j]
        )

    def finish(j, state):
        out_own[:, strip_of(j)] = (state[0] / state[1]).astype(BF16)
        out_copy(j).start()

    def arrived(slots, j, parts=(0, 1)):
        for slot in slots:
            for t in parts:
                strip_copy(slot, t, j).wait_recv()

    def pass_on(step):
        for flow in range(2):

            @pl.when(jnp.logical_and(is_relay[flow], step == HOP_STEP[flow] + lax.div(3 * piece[flow], 8)))
            def _():
                piece_copy(flow, 0).wait_recv()
                hop_copy(flow).start()

    @pl.loop(0, strips)
    def _(j):
        arrived([SAME], j)
        keep(j, attend([4, SAME], j))

        @pl.when(jnp.logical_and(core == 0, j == 0))
        def _():
            pl.semaphore_wait(off_ready, 1)
            start_off()

        @pl.when(jnp.logical_and(first, j == 0))
        def _():
            pl.semaphore_wait(ready, RELAYS)
            start_pieces(1)

        pass_on(j)

    for slot in (UP, DOWN, OFF):
        len_copy(slot).wait_recv()
        take_mask(slot)

    @pl.loop(0, strips - 1)
    def _(j):
        arrived([OFF, UP, DOWN], j)
        finish(j, merged(j, *attend([OFF, UP, DOWN], j)))
        pass_on(strips + j)

    end = strips - 1
    arrived([OFF], end)
    keep(end, merged(end, *attend([OFF], end)))
    arrived([UP, DOWN], end, (0,))
    take_keys([UP, DOWN], end)
    tops = []
    for head, scores in enumerate([score(head, 2, end) for head in range(2)]):
        probs[head], top = weigh(scores)
        tops.append(top)
    arrived([UP, DOWN], end, (1,))
    take_values([UP, DOWN], end)
    pair = [blend(head, 2, probs[head]) for head in range(2)]
    finish(end, merged(end, *joined(pair, tops)))

    for slot in range(4):
        len_copy(slot).wait_send()
    for j in range(strips):
        for slot in (UP, DOWN, SAME):
            for t in range(2):
                strip_copy(slot, t, j).wait_send()

        @pl.when(inner)
        def _():
            for t in range(2):
                strip_copy(OFF, t, j).wait_send()

    for flow in range(2):

        @pl.when(is_relay[flow])
        def _():
            hop_copy(flow).wait_send()

    @pl.when(jnp.logical_not(inner))
    def _():
        for g in range(RELAYS):
            piece_copy(0, g).wait_send()

    for j in range(strips):
        out_copy(j).wait()


def local(count, queries, keys, values, lengths):
    rows, width = queries.shape
    strips = width // LANES
    hbm = pl.BlockSpec(memory_space=pl.ANY)
    dma = pltpu.SemaphoreType.DMA
    return pl.pallas_call(
        functools.partial(kernel, count),
        out_shape=jax.ShapeDtypeStruct((rows, width), BF16),
        in_specs=[pl.BlockSpec(memory_space=pltpu.SMEM), hbm, hbm, hbm],
        out_specs=hbm,
        scratch_shapes=[
            pltpu.VMEM((rows, width), BF16),
            pltpu.VMEM((2, rows, width), BF16),
            pltpu.VMEM((4, 2, rows, width), BF16),
            pltpu.VMEM((rows, width), BF16),
            pltpu.VMEM((5, 8, LANES), jnp.int32),
            pltpu.VMEM((5, rows, LANES), BF16),
            pltpu.VMEM((2, 3 * rows, LANES), BF16),
            pltpu.VMEM((2, 3 * rows, LANES), BF16),
            pltpu.VMEM((2, rows, 2 * rows), BF16),
            pltpu.VMEM((strips, rows, LANES), F32),
            pltpu.VMEM((strips, rows, LANES), F32),
            pltpu.VMEM((strips, rows, LANES), F32),
            pltpu.VMEM((2, rows, LANES), BF16),
            dma((3,)),
            dma((4, 2, strips)),
            dma((4, 2, strips)),
            dma((4,)),
            dma((4,)),
            dma((RELAYS,)),
            dma((2,)),
            dma((2,)),
            dma((strips,)),
            pltpu.SemaphoreType.REGULAR,
            pltpu.SemaphoreType.REGULAR,
        ],
        compiler_params=pltpu.CompilerParams(
            collective_id=0, has_side_effects=True, vmem_limit_bytes=56 << 20
        ),
        cost_estimate=pl.CostEstimate(
            flops=20 * rows * rows * width, bytes_accessed=12 * rows * width, transcendentals=80 * rows * rows
        ),
    )(lengths, queries, keys, values)


def solution(mesh):
    return jax.shard_map(
        functools.partial(local, mesh.shape["seq"]),
        mesh=mesh,
        in_specs=(P("seq", None), P("seq", None), P("seq", None), P("seq")),
        out_specs=P("seq", None),
        check_vma=False,
    )
```

```python
import functools
import math

import jax
import jax.numpy as jnp
from jax import lax
from jax.experimental import pallas as pl
from jax.experimental.pallas import tpu as pltpu
from jax.sharding import PartitionSpec as P

MESH = pl.DeviceIdType.MESH
HEAD_DIM = 64
LANES = 128
PLANE = 128
RELAYS = 16
HOP_STEP = (5, 4)
UP, DOWN, SAME, OFF = range(4)
GAIN = math.log2(math.e) / math.sqrt(HEAD_DIM)
BF16 = jnp.bfloat16
F32 = jnp.float32


RELAY_AT = (
    (2, 1, 1), (5, 1, 1), (7, 6, 1), (6, 0, 1), (1, 0, 1), (6, 6, 1), (7, 5, 1), (4, 1, 1),
    (0, 0, 1), (5, 0, 1), (0, 1, 1), (5, 6, 1), (2, 0, 1), (6, 1, 1), (3, 0, 1), (4, 0, 1),
)


def relay_place(flow, g):
    y, z, core = RELAY_AT[g]
    place = (y * 8 + z) * 2 + core
    return place if flow == 0 else PLANE - 1 - place


def kernel(
    count, len_ref, q_hbm, k_hbm, v_hbm, out_ref,
    q_own, kv_own, kv_in, lens, bias, k_aug, v_aug, probs, acc, tot, peak, relay,
    own_sem, send_sem, recv_sem, len_send, len_recv, piece_sem, hop_recv, hop_send, ready, off_ready, hop_ready,
):
    rows, width = q_own.shape
    strips = width // LANES
    me = lax.axis_index("seq")
    core = lax.rem(me, 2)
    place = lax.rem(me, PLANE)
    plane = me - place
    above = lax.rem(plane + PLANE, count)
    below = lax.rem(plane + count - PLANE, count)
    partners = [
        lax.rem(me + PLANE, count),
        lax.rem(me + count - PLANE, count),
        me + 1 - 2 * core,
        lax.rem(me + count - 1 + 2 * core, count),
    ]
    first, last = place == 0, place == PLANE - 1
    inner = jnp.logical_not(jnp.logical_or(first, last))
    is_relay, piece = [], []
    for flow in range(2):
        hits = [place == relay_place(flow, g) for g in range(RELAYS)]
        is_relay.append(functools.reduce(jnp.logical_or, hits))
        piece.append(sum(jnp.where(hit, g, 0) for g, hit in enumerate(hits)))

    def strip_of(j):
        if isinstance(j, int):
            return pl.ds(j * LANES, LANES)
        return pl.ds(pl.multiple_of(j * LANES, LANES), LANES)

    def remote(src, dst, send, recv, device):
        return pltpu.make_async_remote_copy(
            src_ref=src, dst_ref=dst, send_sem=send, recv_sem=recv, device_id=(device,), device_id_type=MESH
        )

    def strip_copy(slot, t, j):
        src = (k_hbm, v_hbm)[t]
        return remote(
            src.at[:, strip_of(j)], kv_in.at[slot, t, :, strip_of(j)],
            send_sem.at[slot, t, j], recv_sem.at[slot, t, j], partners[slot],
        )

    def len_copy(slot):
        return remote(lens.at[4], lens.at[slot], len_send.at[slot], len_recv.at[slot], partners[slot])

    def piece_copy(flow, g):
        src = (k_hbm, v_hbm)[g % 2]
        return remote(
            src.at[:, strip_of(g // 2)], relay.at[flow], piece_sem.at[g], hop_recv.at[flow],
            (above, below)[flow] + relay_place(flow, g),
        )

    def hop_copy(flow):
        t, j = lax.rem(piece[flow], 2), lax.div(piece[flow], 2)
        return remote(
            relay.at[flow], kv_in.at[OFF, t, :, strip_of(j)], hop_send.at[flow], recv_sem.at[OFF, t, j],
            plane + (0, PLANE - 1)[flow],
        )

    def signal(semaphore, device):
        pl.semaphore_signal(semaphore, inc=1, device_id=(device,), device_id_type=MESH)

    local = [
        pltpu.make_async_copy(q_hbm, q_own, own_sem.at[0]),
        pltpu.make_async_copy(k_hbm, kv_own.at[0], own_sem.at[1]),
        pltpu.make_async_copy(v_hbm, kv_own.at[1], own_sem.at[2]),
    ]
    barrier = pltpu.get_barrier_semaphore()
    for slot in (UP, DOWN, SAME):
        signal(barrier, partners[slot])

    @pl.when(core == 0)
    def _():
        signal(barrier, partners[OFF])

    @pl.when(first)
    def _():
        for g in range(RELAYS):
            signal(barrier, plane + relay_place(0, g))
            signal(barrier, below + relay_place(1, g))

    @pl.when(is_relay[0])
    def _():
        signal(barrier, below + PLANE - 1)

    @pl.when(is_relay[1])
    def _():
        signal(barrier, plane + PLANE - 1)

    for copy in local:
        copy.start()
    lens[4] = jnp.full(lens.shape[1:], len_ref[0], jnp.int32)
    pl.semaphore_wait(
        barrier,
        3 + core + jnp.where(last, 2 * RELAYS, 0) + sum(jnp.where(hit, 1, 0) for hit in is_relay),
    )

    @pl.when(core == 1)
    def _():
        signal(off_ready, partners[OFF])

    @pl.when(is_relay[1])
    def _():
        signal(ready, above)

    @pl.when(last)
    def _():
        for g in range(RELAYS):
            signal(hop_ready, plane + relay_place(1, g))

    def start_pieces(flow):
        for g in range(RELAYS):
            piece_copy(flow, g).start()

    def start_off():
        len_copy(OFF).start()

        @pl.when(inner)
        def _():
            for j in range(strips):
                for t in range(2):
                    strip_copy(OFF, t, j).start()

    pl.when(last)(functools.partial(start_pieces, 0))
    for slot in (UP, DOWN, SAME):
        len_copy(slot).start()
    for j in range(strips):
        for slot in (UP, DOWN, SAME):
            for t in range(2):
                strip_copy(slot, t, j).start()
    pl.when(core == 1)(start_off)

    for copy in local:
        copy.wait()
    position = lax.broadcasted_iota(jnp.int32, (rows, LANES), 0)

    def take_mask(block):
        bias[block] = jnp.where(position < lens[block, 0:1, :], 0.0, -1e30).astype(BF16)

    take_mask(4)
    len_copy(SAME).wait_recv()
    take_mask(SAME)

    lane = lax.broadcasted_iota(jnp.int32, (rows, LANES), 1)
    low = lane < HEAD_DIM
    ones = jnp.ones((rows, LANES), BF16)
    marks = ((lane == HEAD_DIM).astype(BF16), (lane == 0).astype(BF16))

    def block_view(block, t, j):
        return kv_own[t, :, strip_of(j)] if block == 4 else kv_in[block, t, :, strip_of(j)]

    def take_keys(blocks, j):
        for i, block in enumerate(blocks):
            keys, mask = block_view(block, 0, j), bias[block]
            at = pl.ds(i * rows, rows)
            k_aug[0, at] = jnp.where(low, keys, mask)
            k_aug[1, at] = jnp.where(low, mask, keys)

    def take_values(blocks, j):
        for i, block in enumerate(blocks):
            values = block_view(block, 1, j)
            at = pl.ds(i * rows, rows)
            v_aug[0, at] = jnp.where(low, values, ones)
            v_aug[1, at] = jnp.where(low, ones, values)

    def score(head, n, j):
        q = q_own[:, strip_of(j)]
        q = jnp.where(low, q, marks[0]) if head == 0 else jnp.where(low, marks[1], q)
        return lax.dot_general(
            q, k_aug[head, 0 : n * rows], (((1,), (1,)), ((), ())), preferred_element_type=F32
        )

    def weigh(scores):
        top = jnp.max(scores, axis=1, keepdims=True)
        return jnp.exp2((scores - top) * GAIN).astype(BF16), top

    def blend(head, n, weights):
        return jnp.dot(weights, v_aug[head, 0 : n * rows], preferred_element_type=F32)

    def joined(pair, tops):
        blended = jnp.where(low, pair[0], pair[1])
        totals = pltpu.roll(jnp.where(low, pair[1], pair[0]), HEAD_DIM, 1)
        return blended, totals, jnp.where(low, tops[0], tops[1])

    def attend(blocks, j):
        take_keys(blocks, j)
        take_values(blocks, j)
        n = len(blocks)
        scores = [score(head, n, j) for head in range(2)]
        weights, tops = zip(*[weigh(s) for s in scores])
        return joined([blend(head, n, weights[head]) for head in range(2)], tops)

    def merged(j, blended, totals, top):
        ceiling = jnp.maximum(peak[j], top)
        old, new = jnp.exp2((peak[j] - ceiling) * GAIN), jnp.exp2((top - ceiling) * GAIN)
        return acc[j] * old + blended * new, tot[j] * old + totals * new, ceiling

    def keep(j, state):
        acc[j], tot[j], peak[j] = state

    def finish(j, state):
        out_ref[:, strip_of(j)] = (state[0] / state[1]).astype(BF16)

    def arrived(slots, j, parts=(0, 1)):
        for slot in slots:
            for t in parts:
                strip_copy(slot, t, j).wait_recv()

    def pass_on(step):
        for flow in range(2):

            @pl.when(jnp.logical_and(is_relay[flow], step == HOP_STEP[flow] + lax.div(3 * piece[flow], 8)))
            def _():
                piece_copy(flow, 0).wait_recv()
                if flow == 1:
                    pl.semaphore_wait(hop_ready, 1)
                hop_copy(flow).start()

    @pl.loop(0, strips)
    def _(j):
        arrived([SAME], j)
        keep(j, attend([4, SAME], j))

        @pl.when(jnp.logical_and(core == 0, j == 0))
        def _():
            pl.semaphore_wait(off_ready, 1)
            start_off()

        @pl.when(jnp.logical_and(first, j == 0))
        def _():
            pl.semaphore_wait(ready, RELAYS)
            start_pieces(1)

        pass_on(j)

    for slot in (UP, DOWN, OFF):
        len_copy(slot).wait_recv()
        take_mask(slot)

    @pl.loop(0, strips - 1)
    def _(j):
        arrived([OFF, UP, DOWN], j)
        finish(j, merged(j, *attend([OFF, UP, DOWN], j)))
        pass_on(strips + j)

    end = strips - 1
    arrived([OFF], end)
    keep(end, merged(end, *attend([OFF], end)))
    arrived([UP, DOWN], end, (0,))
    take_keys([UP, DOWN], end)
    tops = []
    for head, scores in enumerate([score(head, 2, end) for head in range(2)]):
        probs[head], top = weigh(scores)
        tops.append(top)
    arrived([UP, DOWN], end, (1,))
    take_values([UP, DOWN], end)
    pair = [blend(head, 2, probs[head]) for head in range(2)]
    finish(end, merged(end, *joined(pair, tops)))

    for slot in range(4):
        len_copy(slot).wait_send()
    for j in range(strips):
        for slot in (UP, DOWN, SAME):
            for t in range(2):
                strip_copy(slot, t, j).wait_send()

        @pl.when(inner)
        def _():
            for t in range(2):
                strip_copy(OFF, t, j).wait_send()

    for flow in range(2):

        @pl.when(is_relay[flow])
        def _():
            hop_copy(flow).wait_send()

    @pl.when(jnp.logical_not(inner))
    def _():
        for g in range(RELAYS):
            piece_copy(0, g).wait_send()


def local(count, queries, keys, values, lengths):
    rows, width = queries.shape
    strips = width // LANES
    hbm = pl.BlockSpec(memory_space=pltpu.HBM)
    dma = pltpu.SemaphoreType.DMA
    return pl.pallas_call(
        functools.partial(kernel, count),
        out_shape=jax.ShapeDtypeStruct((rows, width), BF16),
        in_specs=[pl.BlockSpec(memory_space=pltpu.SMEM), hbm, hbm, hbm],
        out_specs=pl.BlockSpec(memory_space=pltpu.VMEM),
        scratch_shapes=[
            pltpu.VMEM((rows, width), BF16),
            pltpu.VMEM((2, rows, width), BF16),
            pltpu.VMEM((4, 2, rows, width), BF16),
            pltpu.VMEM((5, 8, LANES), jnp.int32),
            pltpu.VMEM((5, rows, LANES), BF16),
            pltpu.VMEM((2, 3 * rows, LANES), BF16),
            pltpu.VMEM((2, 3 * rows, LANES), BF16),
            pltpu.VMEM((2, rows, 2 * rows), BF16),
            pltpu.VMEM((strips, rows, LANES), F32),
            pltpu.VMEM((strips, rows, LANES), F32),
            pltpu.VMEM((strips, rows, LANES), F32),
            pltpu.VMEM((2, rows, LANES), BF16),
            dma((3,)),
            dma((4, 2, strips)),
            dma((4, 2, strips)),
            dma((4,)),
            dma((4,)),
            dma((RELAYS,)),
            dma((2,)),
            dma((2,)),
            pltpu.SemaphoreType.REGULAR,
            pltpu.SemaphoreType.REGULAR,
            pltpu.SemaphoreType.REGULAR,
        ],
        compiler_params=pltpu.CompilerParams(
            collective_id=0, has_side_effects=True, vmem_limit_bytes=52 << 20
        ),
        cost_estimate=pl.CostEstimate(
            flops=20 * rows * rows * width, bytes_accessed=12 * rows * width, transcendentals=80 * rows * rows
        ),
    )(lengths, queries, keys, values)


def solution(mesh):
    return jax.shard_map(
        functools.partial(local, mesh.shape["seq"]),
        mesh=mesh,
        in_specs=(P("seq", None), P("seq", None), P("seq", None), P("seq")),
        out_specs=P("seq", None),
        check_vma=False,
    )
```

```python
import functools
import math

import jax
import jax.numpy as jnp
from jax import lax
from jax.experimental import pallas as pl
from jax.experimental.pallas import tpu as pltpu
from jax.sharding import PartitionSpec as P

MESH = pl.DeviceIdType.MESH
HEAD_DIM = 64
LANES = 128
PLANE = 128
RELAYS = 16
HOP_STEP = (5, 4)
UP, DOWN, SAME, OFF = range(4)
GAIN = math.log2(math.e) / math.sqrt(HEAD_DIM)
BF16 = jnp.bfloat16
F32 = jnp.float32


RELAY_AT = (
    (2, 1, 1), (5, 1, 1), (7, 6, 1), (6, 0, 1), (1, 0, 1), (6, 6, 1), (7, 5, 1), (4, 1, 1),
    (0, 0, 1), (5, 0, 1), (0, 1, 1), (5, 6, 1), (2, 0, 1), (6, 1, 1), (3, 0, 1), (4, 0, 1),
)


def relay_place(flow, g):
    y, z, core = RELAY_AT[g]
    place = (y * 8 + z) * 2 + core
    return place if flow == 0 else PLANE - 1 - place


def kernel(
    count, len_ref, q_hbm, k_hbm, v_hbm, out_ref,
    q_own, kv_own, kv_in, lens, bias, k_aug, v_aug, probs, acc, tot, peak, relay,
    own_sem, send_sem, recv_sem, len_send, len_recv, piece_sem, hop_recv, hop_send, ready, off_ready, hop_ready,
):
    rows, width = q_own.shape
    strips = width // LANES
    me = lax.axis_index("seq")
    core = lax.rem(me, 2)
    place = lax.rem(me, PLANE)
    plane = me - place
    above = lax.rem(plane + PLANE, count)
    below = lax.rem(plane + count - PLANE, count)
    partners = [
        lax.rem(me + PLANE, count),
        lax.rem(me + count - PLANE, count),
        me + 1 - 2 * core,
        lax.rem(me + count - 1 + 2 * core, count),
    ]
    first, last = place == 0, place == PLANE - 1
    inner = jnp.logical_not(jnp.logical_or(first, last))
    is_relay, piece = [], []
    for flow in range(2):
        hits = [place == relay_place(flow, g) for g in range(RELAYS)]
        is_relay.append(functools.reduce(jnp.logical_or, hits))
        piece.append(sum(jnp.where(hit, g, 0) for g, hit in enumerate(hits)))

    def strip_of(j):
        if isinstance(j, int):
            return pl.ds(j * LANES, LANES)
        return pl.ds(pl.multiple_of(j * LANES, LANES), LANES)

    def remote(src, dst, send, recv, device):
        return pltpu.make_async_remote_copy(
            src_ref=src, dst_ref=dst, send_sem=send, recv_sem=recv, device_id=(device,), device_id_type=MESH
        )

    def strip_copy(slot, t, j):
        src = (k_hbm, v_hbm)[t]
        return remote(
            src.at[:, strip_of(j)], kv_in.at[slot, t, :, strip_of(j)],
            send_sem.at[slot, t, j], recv_sem.at[slot, t, j], partners[slot],
        )

    def wide_copy(slot, t, j):
        src = (k_hbm, v_hbm)[t]
        lanes = pl.ds(j * LANES if isinstance(j, int) else pl.multiple_of(j * LANES, LANES), 2 * LANES)
        return remote(
            src.at[:, lanes], kv_in.at[slot, t, :, lanes],
            send_sem.at[slot, t, j], recv_sem.at[slot, t, j], partners[slot],
        )

    def len_copy(slot):
        return remote(lens.at[4], lens.at[slot], len_send.at[slot], len_recv.at[slot], partners[slot])

    def piece_copy(flow, g):
        src = (k_hbm, v_hbm)[g % 2]
        return remote(
            src.at[:, strip_of(g // 2)], relay.at[flow], piece_sem.at[g], hop_recv.at[flow],
            (above, below)[flow] + relay_place(flow, g),
        )

    def hop_copy(flow):
        t, j = lax.rem(piece[flow], 2), lax.div(piece[flow], 2)
        return remote(
            relay.at[flow], kv_in.at[OFF, t, :, strip_of(j)], hop_send.at[flow], recv_sem.at[OFF, t, j],
            plane + (0, PLANE - 1)[flow],
        )

    def signal(semaphore, device):
        pl.semaphore_signal(semaphore, inc=1, device_id=(device,), device_id_type=MESH)

    local = [
        pltpu.make_async_copy(q_hbm, q_own, own_sem.at[0]),
        pltpu.make_async_copy(k_hbm, kv_own.at[0], own_sem.at[1]),
        pltpu.make_async_copy(v_hbm, kv_own.at[1], own_sem.at[2]),
    ]
    barrier = pltpu.get_barrier_semaphore()
    for slot in (UP, DOWN, SAME):
        signal(barrier, partners[slot])

    @pl.when(core == 0)
    def _():
        signal(barrier, partners[OFF])

    @pl.when(first)
    def _():
        for g in range(RELAYS):
            signal(barrier, plane + relay_place(0, g))
            signal(barrier, below + relay_place(1, g))

    @pl.when(is_relay[0])
    def _():
        signal(barrier, below + PLANE - 1)

    @pl.when(is_relay[1])
    def _():
        signal(barrier, plane + PLANE - 1)

    for copy in local:
        copy.start()
    lens[4] = jnp.full(lens.shape[1:], len_ref[0], jnp.int32)
    pl.semaphore_wait(
        barrier,
        3 + core + jnp.where(last, 2 * RELAYS, 0) + sum(jnp.where(hit, 1, 0) for hit in is_relay),
    )

    @pl.when(core == 1)
    def _():
        signal(off_ready, partners[OFF])

    @pl.when(is_relay[1])
    def _():
        signal(ready, above)

    @pl.when(last)
    def _():
        for g in range(RELAYS):
            signal(hop_ready, plane + relay_place(1, g))

    def start_pieces(flow):
        for g in range(RELAYS):
            piece_copy(flow, g).start()

    def start_off():
        len_copy(OFF).start()

        @pl.when(inner)
        def _():
            for j in range(strips):
                for t in range(2):
                    strip_copy(OFF, t, j).start()

    pl.when(last)(functools.partial(start_pieces, 0))
    for slot in (UP, DOWN, SAME):
        len_copy(slot).start()
    for j in range(strips):
        for t in range(2):
            strip_copy(SAME, t, j).start()
        for slot in (UP, DOWN):
            for t in range(2):
                if j >= strips - 2:
                    strip_copy(slot, t, j).start()
                elif j % 2 == 0:
                    wide_copy(slot, t, j).start()
    pl.when(core == 1)(start_off)

    for copy in local:
        copy.wait()
    position = lax.broadcasted_iota(jnp.int32, (rows, LANES), 0)

    def take_mask(block):
        bias[block] = jnp.where(position < lens[block, 0:1, :], 0.0, -1e30).astype(BF16)

    take_mask(4)
    len_copy(SAME).wait_recv()
    take_mask(SAME)

    lane = lax.broadcasted_iota(jnp.int32, (rows, LANES), 1)
    low = lane < HEAD_DIM
    ones = jnp.ones((rows, LANES), BF16)
    marks = ((lane == HEAD_DIM).astype(BF16), (lane == 0).astype(BF16))

    def block_view(block, t, j):
        return kv_own[t, :, strip_of(j)] if block == 4 else kv_in[block, t, :, strip_of(j)]

    def take_keys(blocks, j):
        for i, block in enumerate(blocks):
            keys, mask = block_view(block, 0, j), bias[block]
            at = pl.ds(i * rows, rows)
            k_aug[0, at] = jnp.where(low, keys, mask)
            k_aug[1, at] = jnp.where(low, mask, keys)

    def take_values(blocks, j):
        for i, block in enumerate(blocks):
            values = block_view(block, 1, j)
            at = pl.ds(i * rows, rows)
            v_aug[0, at] = jnp.where(low, values, ones)
            v_aug[1, at] = jnp.where(low, ones, values)

    def score(head, n, j):
        q = q_own[:, strip_of(j)]
        q = jnp.where(low, q, marks[0]) if head == 0 else jnp.where(low, marks[1], q)
        return lax.dot_general(
            q, k_aug[head, 0 : n * rows], (((1,), (1,)), ((), ())), preferred_element_type=F32
        )

    def weigh(scores):
        top = jnp.max(scores, axis=1, keepdims=True)
        return jnp.exp2((scores - top) * GAIN).astype(BF16), top

    def blend(head, n, weights):
        return jnp.dot(weights, v_aug[head, 0 : n * rows], preferred_element_type=F32)

    def joined(pair, tops):
        blended = jnp.where(low, pair[0], pair[1])
        totals = pltpu.roll(jnp.where(low, pair[1], pair[0]), HEAD_DIM, 1)
        return blended, totals, jnp.where(low, tops[0], tops[1])

    def attend(blocks, j):
        take_keys(blocks, j)
        take_values(blocks, j)
        n = len(blocks)
        scores = [score(head, n, j) for head in range(2)]
        weights, tops = zip(*[weigh(s) for s in scores])
        return joined([blend(head, n, weights[head]) for head in range(2)], tops)

    def merged(j, blended, totals, top):
        ceiling = jnp.maximum(peak[j], top)
        old, new = jnp.exp2((peak[j] - ceiling) * GAIN), jnp.exp2((top - ceiling) * GAIN)
        return acc[j] * old + blended * new, tot[j] * old + totals * new, ceiling

    def keep(j, state):
        acc[j], tot[j], peak[j] = state

    def finish(j, state):
        out_ref[:, strip_of(j)] = (state[0] / state[1]).astype(BF16)

    def arrived(slots, j, parts=(0, 1)):
        for slot in slots:
            for t in parts:
                strip_copy(slot, t, j).wait_recv()

    def pass_on(step):
        for flow in range(2):

            @pl.when(jnp.logical_and(is_relay[flow], step == HOP_STEP[flow] + lax.div(3 * piece[flow], 8)))
            def _():
                piece_copy(flow, 0).wait_recv()
                if flow == 1:
                    pl.semaphore_wait(hop_ready, 1)
                hop_copy(flow).start()

    @pl.loop(0, strips)
    def _(j):
        arrived([SAME], j)
        keep(j, attend([4, SAME], j))

        @pl.when(jnp.logical_and(core == 0, j == 0))
        def _():
            pl.semaphore_wait(off_ready, 1)
            start_off()

        @pl.when(jnp.logical_and(first, j == 0))
        def _():
            pl.semaphore_wait(ready, RELAYS)
            start_pieces(1)

        pass_on(j)

    for slot in (UP, DOWN, OFF):
        len_copy(slot).wait_recv()
        take_mask(slot)

    @pl.loop(0, strips - 1)
    def _(j):
        arrived([OFF], j)

        @pl.when(jnp.logical_and(lax.rem(j, 2) == 0, j < strips - 2))
        def _():
            for slot in (UP, DOWN):
                for t in range(2):
                    wide_copy(slot, t, j).wait_recv()

        @pl.when(j == strips - 2)
        def _():
            arrived([UP, DOWN], strips - 2)

        finish(j, merged(j, *attend([OFF, UP, DOWN], j)))
        pass_on(strips + j)

    end = strips - 1
    arrived([OFF], end)
    keep(end, merged(end, *attend([OFF], end)))
    arrived([UP, DOWN], end, (0,))
    take_keys([UP, DOWN], end)
    tops = []
    for head, scores in enumerate([score(head, 2, end) for head in range(2)]):
        probs[head], top = weigh(scores)
        tops.append(top)
    arrived([UP, DOWN], end, (1,))
    take_values([UP, DOWN], end)
    pair = [blend(head, 2, probs[head]) for head in range(2)]
    finish(end, merged(end, *joined(pair, tops)))

    for slot in range(4):
        len_copy(slot).wait_send()
    for j in range(strips):
        for t in range(2):
            strip_copy(SAME, t, j).wait_send()
        for slot in (UP, DOWN):
            for t in range(2):
                if j >= strips - 2:
                    strip_copy(slot, t, j).wait_send()
                elif j % 2 == 0:
                    wide_copy(slot, t, j).wait_send()

        @pl.when(inner)
        def _():
            for t in range(2):
                strip_copy(OFF, t, j).wait_send()

    for flow in range(2):

        @pl.when(is_relay[flow])
        def _():
            hop_copy(flow).wait_send()

    @pl.when(jnp.logical_not(inner))
    def _():
        for g in range(RELAYS):
            piece_copy(0, g).wait_send()


def local(count, queries, keys, values, lengths):
    rows, width = queries.shape
    strips = width // LANES
    hbm = pl.BlockSpec(memory_space=pltpu.HBM)
    dma = pltpu.SemaphoreType.DMA
    return pl.pallas_call(
        functools.partial(kernel, count),
        out_shape=jax.ShapeDtypeStruct((rows, width), BF16),
        in_specs=[pl.BlockSpec(memory_space=pltpu.SMEM), hbm, hbm, hbm],
        out_specs=pl.BlockSpec(memory_space=pltpu.VMEM),
        scratch_shapes=[
            pltpu.VMEM((rows, width), BF16),
            pltpu.VMEM((2, rows, width), BF16),
            pltpu.VMEM((4, 2, rows, width), BF16),
            pltpu.VMEM((5, 8, LANES), jnp.int32),
            pltpu.VMEM((5, rows, LANES), BF16),
            pltpu.VMEM((2, 3 * rows, LANES), BF16),
            pltpu.VMEM((2, 3 * rows, LANES), BF16),
            pltpu.VMEM((2, rows, 2 * rows), BF16),
            pltpu.VMEM((strips, rows, LANES), F32),
            pltpu.VMEM((strips, rows, LANES), F32),
            pltpu.VMEM((strips, rows, LANES), F32),
            pltpu.VMEM((2, rows, LANES), BF16),
            dma((3,)),
            dma((4, 2, strips)),
            dma((4, 2, strips)),
            dma((4,)),
            dma((4,)),
            dma((RELAYS,)),
            dma((2,)),
            dma((2,)),
            pltpu.SemaphoreType.REGULAR,
            pltpu.SemaphoreType.REGULAR,
            pltpu.SemaphoreType.REGULAR,
        ],
        compiler_params=pltpu.CompilerParams(
            collective_id=0, has_side_effects=True, vmem_limit_bytes=52 << 20
        ),
        cost_estimate=pl.CostEstimate(
            flops=20 * rows * rows * width, bytes_accessed=12 * rows * width, transcendentals=80 * rows * rows
        ),
    )(lengths, queries, keys, values)


def solution(mesh):
    return jax.shard_map(
        functools.partial(local, mesh.shape["seq"]),
        mesh=mesh,
        in_specs=(P("seq", None), P("seq", None), P("seq", None), P("seq")),
        out_specs=P("seq", None),
        check_vma=False,
    )
```
